256 devices in a mesh: row: 4 (over x), col: 64 (over y, z, core).
Axes of the slice: x: 4, y: 4, z: 8, core: 2. Of those that a mesh axis runs over, the one named last changes fastest.
Arguments:
- left_image: float32 [256, 16384], P('row', 'col'), may hold values from -6 to 6
- right_image: float32 [256, 16384], P('row', 'col'), may hold values from -6 to 6
Outputs:
- aggregated: float32 [256, 16384, 128], P('row', 'col')
The draws below stay inside these ranges and needn't reach their ends.
All inputs are finite; a program needn't handle non-finite values.
Results may differ from the reference program's by a relative error of at most 0.0003.
Values sent between devices are 32-bit elements; how exact they have to be, the bound alone decides.
No kernel may reach another device: no remote copies, remote signals or barrier semaphores. Data moves between devices by JAX's collectives and lax.ppermute only.
A program may use at most 128 MiB of HBM per device.

```python
import jax
import jax.numpy as jnp
from jax import lax

ND = 128
H = 256
W = 16384


def steps_of(key, shape, cuts, least, high):
    gain, own = 1.0, jax.random.fold_in(key, 6)
    for position, blocks in cuts:
        draws = jnp.exp(jax.random.uniform(jax.random.fold_in(own, position), (blocks,), jnp.float32, least / len(cuts), high / len(cuts)))
        gain = gain * jnp.repeat(draws, shape[position] // blocks).reshape([-1 if axis == position else 1 for axis in range(len(shape))])
    return gain


def noise(rng, dims, spread, most, pieces=(), held_as=jnp.bfloat16):
    gain = steps_of(rng, dims, pieces, -0.22, 0.18) if pieces else 1.0
    drawn = jax.random.normal(rng, dims, jnp.float32) * spread * gain
    return jnp.minimum(jnp.maximum(drawn, -most), most).astype(held_as)


def setup_inputs(seed: int = 0) -> dict:
    keys = jax.random.split(jax.random.key(seed), 3)
    left_image = noise(keys[0], (H, W), 1.0, 6.0, ((0, 4), (1, 64)), jnp.float32)
    right_image = noise(keys[1], (H, W), 1.0, 6.0, ((0, 4), (1, 64)), jnp.float32)
    return dict(left_image=left_image, right_image=right_image)


def reference(left_image, right_image):
    rows, cols = left_image.shape
    right_pad = jnp.pad(right_image, ((0, 0), (ND, 0)))

    def one(disp):
        shifted = lax.dynamic_slice_in_dim(right_pad, (ND - disp).astype(jnp.int32), cols, 1)
        cost = jnp.abs(left_image - shifted)
        padded = jnp.pad(cost, 4)
        summed = padded[0:rows, :]
        for offset in range(1, 9):
            summed = summed + padded[offset:offset + rows, :]
        total = summed[:, 0:cols]
        for offset in range(1, 9):
            total = total + summed[:, offset:offset + cols]
        return total / 81.0

    stacked = lax.map(one, jnp.arange(ND, dtype=jnp.int32))
    return jnp.transpose(stacked, (1, 2, 0))
```

```python
import functools

import jax
import jax.numpy as jnp
from jax import lax
from jax.experimental import pallas as pl
from jax.experimental.pallas import tpu as pltpu
from jax.sharding import PartitionSpec as P

ND = 128
ROWS = 64
COLS = 256
F32 = jnp.float32
BF16 = jnp.bfloat16
NT = (((1,), (1,)), ((), ()))
SCALE = 1.0 / 81.0
GROUP = 32
VMEM = pl.BlockSpec(memory_space=pltpu.VMEM)
HBM = pl.BlockSpec(memory_space=pl.ANY)


def iota(shape, dim):
    return lax.broadcasted_iota(jnp.int32, shape, dim)


def tile(ref, t):
    return ref[:, 128 * t : 128 * t + 128]


def one_hot(mask):
    return jnp.where(mask, 1.0, 0.0).astype(BF16)


def halves(x):
    high = x.astype(BF16)
    low = (x - high.astype(F32)).astype(BF16)
    return jnp.concatenate([high, low], axis=1)


def pick_transposed(chosen, x):
    a = x.astype(BF16)
    rest = x - a.astype(F32)
    b = rest.astype(BF16)
    c = (rest - b.astype(F32)).astype(BF16)
    dot = functools.partial(lax.dot_general, dimension_numbers=NT, preferred_element_type=F32)
    return (dot(chosen, c) + dot(chosen, b)) + dot(chosen, a)


def side_tiles(cross, intra):
    c = lax.axis_index("col")
    odd = (c % 2) == 1
    west = jnp.where(odd, intra, cross)
    east = jnp.where(odd, cross, intra)
    west = jnp.where(c == 0, 0.0, west)
    east = jnp.where(c == lax.axis_size("col") - 1, 0.0, east)
    lane = iota((west.shape[0], 128), 1)
    right_far = west[:, 0:128]
    right_edge = jnp.where(lane < 4, east[:, 128:256], west[:, 128:256])
    left_edge = pltpu.roll(jnp.where(lane >= 8, east[:, 128:256], west[:, 128:256]), 120, 1)
    return right_far, right_edge, left_edge


def pack_kernel(left, right, out):
    lane = iota((ROWS, 128), 1)
    edge = pltpu.roll(jnp.where(lane >= 124, tile(left, 1), tile(left, 0)), 8, 1)
    out[:, 0:128] = tile(right, 1)
    out[:, 128:256] = jnp.where((lane >= 4) & (lane < 12), edge, tile(right, 0))


def rows_kernel(left, right, cross, intra, out1, out2):
    odd = (lax.axis_index("row") % 2) == 1

    def strip(first):
        rows = pl.ds(first, 8)
        far, right_edge, left_edge = side_tiles(cross[rows, :], intra[rows, :])
        return jnp.concatenate([right_edge, far, right[rows, :], left_edge, left[rows, :]], axis=1)

    top, bottom = strip(0), strip(ROWS - 8)
    out1[...] = jnp.where(odd, top, bottom)
    out2[...] = jnp.where(odd, bottom, top)


def spread(tmp, pieces, store):
    size = pieces[0].shape[0]
    for t, piece in enumerate(pieces):
        tmp[pl.ds((size + 1) * t, size), :] = piece
    for u in range(len(pieces) // 8):
        for r in range(size):
            store(r, 8 * u, tmp[pl.ds((size + 1) * 8 * u + r, 8, stride=size + 1), :])


def block_kernel(left, right, cross, intra, out, edges, rr, lr, ob, tmp, sem):
    last = lax.axis_index("col") == lax.axis_size("col") - 1
    lane = iota((ROWS, 128), 1)
    far, right_edge, left_edge = side_tiles(cross[...], intra[...])
    r0, r1, l0, l1 = tile(right, 0), tile(right, 1), tile(left, 0), tile(left, 1)
    x = jnp.concatenate(
        [
            jnp.concatenate([jnp.where(lane < 4, r1, right_edge), far, r0], axis=1),
            jnp.concatenate([jnp.where(lane < 4, right_edge, far), r0, r1], axis=1),
        ],
        axis=0,
    )
    q, p = iota((264, 384), 0), iota((264, 384), 1)
    col = 131 - q
    rr[...] = pick_transposed(one_hot(p == jnp.where(col >= 128, col - 128, col + 256)), x)
    x = jnp.concatenate(
        [
            jnp.concatenate([jnp.where(lane < 4, l1, left_edge), l0], axis=1),
            jnp.concatenate([jnp.where(lane < 4, left_edge, l0), l1], axis=1),
        ],
        axis=0,
    )
    q, p = iota((136, 256), 0), iota((136, 256), 1)
    col = q - 4
    lr[...] = pick_transposed(one_hot(p == jnp.where(col >= 128, col - 128, col + 128)), x)
    a, b = iota((128, 128), 0), iota((128, 128), 1)
    e = a % 64
    i = jnp.where(e < 4, e, jnp.where(e < 8, e + 56, e - 4))
    band = one_hot(((a // 64) == (b // 64)) & (jnp.abs(i - b % 64) <= 4))
    band = jnp.concatenate([band, band], axis=1)
    half1 = iota((1, 128), 1) >= 64

    def cost(j):
        return jnp.abs(lr[pl.ds(j, 1), :] - rr[pl.ds(135 - j, 128), :])

    def copy(c, h):
        return pltpu.make_async_copy(ob.at[c], out.at[pl.ds(4, ROWS - 8), c, :], sem)

    total = jnp.zeros((128, 128), F32)
    for j in range(8):
        total = total + cost(j)
    steps = 128 // GROUP

    def step(s, total):
        first = s * GROUP
        outside = half1 & last & (s == steps - 1)
        top = [[], []]
        for t in range(GROUP):
            new = cost(first + t + 8)
            if t >= GROUP - 4:
                new = jnp.where(outside, 0.0, new)
            total = total + new
            done = lax.dot_general(band, halves(total), NT, preferred_element_type=F32) * SCALE
            total = total - cost(first + t)
            for h in range(2):
                c = 128 * h + first + t
                top[h].append(done[64 * h : 64 * h + 8])
                ob[c] = done[64 * h + 8 : 64 * h + 64]
                copy(c, h).start()
        for h in range(2):

            def store(r, u, value):
                edges[r, pl.ds(pl.multiple_of(128 * h + first + u, 8), 8), :] = value

            spread(tmp, top[h], store)
        return total

    lax.fori_loop(0, steps, step, total)

    pltpu.make_async_copy(ob, out.at[pl.ds(0, ROWS - 8)].reshape(COLS, ROWS - 8, 128), sem).wait()


def edge_kernel(x1, x2, partial, alias, out, rr, lr, ob, tmp, sem):
    del alias
    row = lax.axis_index("row")
    odd = (row % 2) == 1
    last = lax.axis_index("col") == lax.axis_size("col") - 1
    north = jnp.where(odd, x1[...], x2[...])
    south = jnp.where(odd, x2[...], x1[...])
    north = jnp.where(row == 0, 0.0, north)
    south = jnp.where(row == lax.axis_size("row") - 1, 0.0, south)
    both = jnp.where(iota((8, 896), 0) >= 4, north, south)
    parts = [both[:, 128 * t : 128 * t + 128] for t in range(7)]
    right = [parts[0], parts[1], parts[2], parts[3], parts[0]]
    left = [parts[4], parts[5], parts[6], parts[4]]
    lane = iota((8, 128), 1)

    def window(tiles, v, o):
        x = jnp.where(lane >= o, tiles[v], tiles[v + 1])
        return pltpu.roll(x, (128 - o) % 128, 1) if o else x

    xr, xl = [], []
    for t in range(16):
        v, o = divmod(16 * t + 120, 128)
        xr.append(jnp.concatenate([window(right, v, o), window(right, v + 1, o)], axis=1))
        v, o = divmod(16 * t + 124, 128)
        xl.append(window(left, v, o))
    q, p = iota((152, 256), 0), iota((152, 256), 1)
    rr[...] = pick_transposed(one_hot(p == 155 - q), jnp.concatenate(xr, axis=0))
    q, p = iota((24, 128), 0), iota((24, 128), 1)
    lr[...] = pick_transposed(one_hot(p == q), jnp.concatenate(xl, axis=0))
    a, b = iota((128, 128), 0), iota((128, 128), 1)
    e, r = a % 8, b % 8
    near = ((e < 4) & (r >= e + 4)) | ((e >= 4) & (r <= e - 4))
    band = one_hot(((a // 8) == (b // 8)) & near)
    band = jnp.concatenate([band, band], axis=1)
    outside = (iota((1, 128), 1) >= 120) & last

    def cost(j):
        return jnp.abs(lr[j : j + 1, :] - rr[23 - j : 151 - j, :])

    total = jnp.zeros((128, 128), F32)
    for j in range(8):
        total = total + cost(j)
    pieces = []
    for t in range(16):
        new = cost(t + 8)
        if t >= 12:
            new = jnp.where(outside, 0.0, new)
        total = total + new
        pieces.append(lax.dot_general(band, halves(total), NT, preferred_element_type=F32) * SCALE)
        total = total - cost(t)

    def store(r, u, value):
        cols = pl.ds(16 * (r // 8) + u, 8)
        ob[r % 8, cols, :] = partial[r % 8, cols, :] + value

    spread(tmp, pieces, store)
    top = pltpu.make_async_copy(ob.at[pl.ds(0, 4)], out.at[pl.ds(0, 4)], sem.at[0])
    bottom = pltpu.make_async_copy(ob.at[pl.ds(4, 4)], out.at[pl.ds(ROWS - 4, 4)], sem.at[1])
    top.start()
    bottom.start()
    top.wait()
    bottom.wait()


def params(mib):
    return pltpu.CompilerParams(vmem_limit_bytes=mib << 20)


def exchange(x, to):
    rows, cols = lax.axis_size("row"), lax.axis_size("col")
    pairs = []
    for r in range(rows):
        for c in range(cols):
            s, d = to(r, c, rows, cols)
            pairs.append((r * cols + c, s * cols + d))
    return lax.ppermute(x, ("row", "col"), pairs)


def across(r, c, rows, cols):
    d = c + 1 if c % 2 else c - 1
    return (r, d) if 0 <= d < cols else (r ^ 1, c)


def within(r, c, rows, cols):
    return r, c ^ 1


def rows_even(r, c, rows, cols):
    return r ^ 1, c


def rows_odd(r, c, rows, cols):
    return (r + 1 if r % 2 else r - 1) % rows, c


def per_device(left, right):
    shape = jax.ShapeDtypeStruct
    packed = pl.pallas_call(
        pack_kernel,
        in_specs=[VMEM, VMEM],
        out_specs=VMEM,
        out_shape=shape((ROWS, COLS), F32),
        name="pack",
    )(left, right)
    cross = exchange(packed, across)
    intra = exchange(packed, within)
    send1, send2 = pl.pallas_call(
        rows_kernel,
        in_specs=[VMEM] * 4,
        out_specs=[VMEM] * 2,
        out_shape=[shape((8, 896), F32)] * 2,
        name="pack_rows",
    )(left, right, cross, intra)
    got1 = exchange(send1, rows_even)
    got2 = exchange(send2, rows_odd)
    out, edges = pl.pallas_call(
        block_kernel,
        in_specs=[VMEM] * 4,
        out_specs=[HBM, VMEM],
        out_shape=[shape((ROWS, COLS, ND), F32), shape((8, COLS, ND), F32)],
        scratch_shapes=[
            pltpu.VMEM((264, 128), F32),
            pltpu.VMEM((136, 128), F32),
            pltpu.VMEM((COLS, ROWS - 8, 128), F32),
            pltpu.VMEM((GROUP * 9 + 8, 128), F32),
            pltpu.SemaphoreType.DMA,
        ],
        compiler_params=params(24),
        cost_estimate=pl.CostEstimate(flops=2 * 128 * 128 * 256 * 128, bytes_accessed=9 << 20, transcendentals=0),
        name="block",
    )(left, right, cross, intra)
    return pl.pallas_call(
        edge_kernel,
        in_specs=[VMEM, VMEM, VMEM, HBM],
        out_specs=HBM,
        out_shape=shape((ROWS, COLS, ND), F32),
        scratch_shapes=[
            pltpu.VMEM((152, 128), F32),
            pltpu.VMEM((24, 128), F32),
            pltpu.VMEM((8, COLS, 128), F32),
            pltpu.VMEM((16 * 129 + 8, 128), F32),
            pltpu.SemaphoreType.DMA((2,)),
        ],
        input_output_aliases={3: 0},
        compiler_params=params(16),
        name="edge",
    )(got1, got2, edges, out)


def solution(mesh):
    specs = (P("row", "col"), P("row", "col"))
    return jax.shard_map(
        per_device, mesh=mesh, in_specs=specs, out_specs=P("row", "col", None), check_vma=False
    )
```

```python
import functools

import jax
import jax.numpy as jnp
from jax import lax
from jax.experimental import pallas as pl
from jax.experimental.pallas import tpu as pltpu
from jax.sharding import PartitionSpec as P

ND = 128
ROWS = 64
COLS = 256
F32 = jnp.float32
BF16 = jnp.bfloat16
NT = (((1,), (1,)), ((), ()))
SCALE = 1.0 / 81.0
LATE = 16
VMEM = pl.BlockSpec(memory_space=pltpu.VMEM)
HBM = pl.BlockSpec(memory_space=pl.ANY)


def iota(shape, dim):
    return lax.broadcasted_iota(jnp.int32, shape, dim)


def tile(ref, t):
    return ref[:, 128 * t : 128 * t + 128]


def one_hot(mask):
    return jnp.where(mask, 1.0, 0.0).astype(BF16)


def halves(x):
    high = x.astype(BF16)
    low = (x - high.astype(F32)).astype(BF16)
    return jnp.concatenate([high, low], axis=1)


def pick_transposed(chosen, x):
    a = x.astype(BF16)
    rest = x - a.astype(F32)
    b = rest.astype(BF16)
    c = (rest - b.astype(F32)).astype(BF16)
    dot = functools.partial(lax.dot_general, dimension_numbers=NT, preferred_element_type=F32)
    return (dot(chosen, c) + dot(chosen, b)) + dot(chosen, a)


def neighbours(cross, intra):
    c = lax.axis_index("col")
    odd = (c % 2) == 1
    west = jnp.where(odd, intra, cross)
    east = jnp.where(odd, cross, intra)
    west = jnp.where(c == 0, 0.0, west)
    east = jnp.where(c == lax.axis_size("col") - 1, 0.0, east)
    return west, east


def turn(x, left):
    left %= 128
    return pltpu.roll(x, 128 - left, 1) if left else x


def side_tiles(west, east, groups):
    far = jnp.concatenate([west[8 * g : 8 * g + 8] for g in groups], axis=0)
    west, east = west[ROWS:], east[ROWS:]
    lane = iota((8, 128), 1)
    both = jnp.where(lane % 16 >= 8, east, west)
    right = [jnp.where(lane < 4, turn(east, 16 * g), turn(west, 16 * g + 16)) for g in groups]
    left = [turn(both, 16 * g + 8) for g in groups]
    return far, jnp.concatenate(right, axis=0), jnp.concatenate(left, axis=0)


def pack_kernel(both, out, images):
    images[...] = both[...]
    lane = iota((8, 128), 1)
    edges = jnp.zeros((8, 128), F32)
    for g in range(ROWS // 8):
        l0, l1, r0, r1 = [images[8 * g : 8 * g + 8, 128 * t : 128 * t + 128] for t in range(4)]
        out[8 * g : 8 * g + 8, :] = r1
        left = turn(jnp.where(lane >= 124, l1, l0), -8)
        some = jnp.where(lane < 4, r0, jnp.where(lane < 12, left, turn(r0, -16)))
        edges = jnp.where(lane // 16 == g, turn(some, -16 * g), edges)
    out[ROWS:, :] = edges


def copy_kernel(x, out):
    out[...] = x[...]


def rows_kernel(images, cross, intra, out1, out2):
    odd = (lax.axis_index("row") % 2) == 1
    west, east = neighbours(cross[...], intra[...])

    def strip(g):
        far, right_edge, left_edge = side_tiles(west, east, [g])
        rows = images[8 * g : 8 * g + 8, :]
        return jnp.concatenate([right_edge, far, rows[:, 256:512], left_edge, rows[:, 0:256]], axis=1)

    top, bottom = strip(0), strip(ROWS // 8 - 1)
    out1[...] = jnp.where(odd, top, bottom)
    out2[...] = jnp.where(odd, bottom, top)


def window(tiles, start):
    v, o = divmod(start, 128)
    if o == 0:
        return tiles[v]
    lane = iota(tiles[v].shape, 1)
    return pltpu.roll(jnp.where(lane >= o, tiles[v], tiles[v + 1]), 128 - o, 1)


def lay_out(right, left, bases, n, rr, lr):
    x = [jnp.concatenate([window(right, b + 120), window(right, b + 248)], axis=1) for b in bases]
    size = -(-(n + 135) // 8) * 8
    q, p = iota((size, 256), 0), iota((size, 256), 1)
    rr[pl.ds(0, size), :] = pick_transposed(one_hot(p == n + 139 - q), jnp.concatenate(x, axis=0))
    x = [window(left, b + 124) for b in bases]
    size = -(-(n + 8) // 8) * 8
    q, p = iota((size, 128), 0), iota((size, 128), 1)
    lr[pl.ds(0, size), :] = pick_transposed(one_hot(p == q), jnp.concatenate(x, axis=0))


def own_band():
    a, b = iota((128, 128), 0), iota((128, 128), 1)
    e = a % 64
    i = jnp.where(e < 4, e, jnp.where(e < 8, e + 56, e - 4))
    band = one_hot(((a // 64) == (b // 64)) & (jnp.abs(i - b % 64) <= 4))
    return jnp.concatenate([band, band], axis=1)


def sweep(rr, lr, ring, band, bases, n, emit, outside=None):
    def cost(j):
        new = jnp.abs(lr[j : j + 1, :] - rr[n + 7 - j : n + 135 - j, :])
        if outside is not None:
            new = outside(j, new)
        if j < n - 1:
            ring[j % 16] = new
        return new

    total = cost(0)
    for j in range(1, 8):
        total = total + cost(j)
    for k in range(n):
        total = total + cost(k + 8)
        emit(k, lax.dot_general(band, halves(total), NT, preferred_element_type=F32) * SCALE)
        if k < n - 1:
            total = total - ring[k % 16]


def columns(segments):
    return [b + k for bases, n, ks in segments for k in ks for b in bases]


INNER = ((132, 192), 60)
OUTER = ((0, 66), 66)
EAST = ((252, 254), 2)
FIRST = [*columns([(*EAST, range(2)), (*OUTER, range(OUTER[1] - LATE))])]
SECOND = columns([(*OUTER, range(OUTER[1] - LATE, OUTER[1]))])
BEFORE = columns([(*INNER, range(INNER[1]))])


def ship(blocks, out, cols, sem):
    for o, c in enumerate(cols):
        pltpu.make_async_copy(blocks.at[o], out.at[pl.ds(4, ROWS - 8), c, :], sem).start()
    return pltpu.make_async_copy(blocks, blocks, sem)


def inner_kernel(images, ready, edges, rr, lr, ring):
    l0, l1, r0, r1 = [tile(images, t) for t in range(4)]
    bases, n = INNER
    lay_out([r0, r0, r0, r1, r1], [l0, l0, l1, l1], bases, n, rr, lr)

    def emit(k, done):
        for h in range(2):
            edges[bases[h] + k] = done[64 * h : 64 * h + 8]
            ready[2 * k + h] = done[64 * h + 8 : 64 * h + 64]

    sweep(rr, lr, ring, own_band(), bases, n, emit)


def outer_kernel(images, cross, intra, ready, part, out, late, edges, rr, lr, rr2, lr2, ring, ob, sem):
    del part
    shipped = ship(ready, out, BEFORE, sem.at[0])
    last = lax.axis_index("col") == lax.axis_size("col") - 1
    far, right_edge, left_edge = side_tiles(*neighbours(cross[...], intra[...]), range(ROWS // 8))
    l0, l1, r0, r1 = [tile(images, t) for t in range(4)]
    rights = [right_edge, far, r0, r1, right_edge]
    lefts = [left_edge, l0, l1, left_edge]
    band = own_band()
    lay_out(rights, lefts, *OUTER, rr, lr)
    lay_out(rights, lefts, *EAST, rr2, lr2)
    lane = iota((1, 128), 1)

    def emit(bases, k, done):
        for h in range(2):
            c = bases[h] + k
            edges[c] = done[64 * h : 64 * h + 8]
            block = done[64 * h + 8 : 64 * h + 64]
            if c in SECOND:
                late[SECOND.index(c)] = block
            else:
                o = FIRST.index(c)
                ob[o] = block
                pltpu.make_async_copy(ob.at[o], out.at[pl.ds(4, ROWS - 8), c, :], sem.at[1]).start()

    def outside(j, new):
        if j < 6:
            return new
        return jnp.where(last & (lane >= 0 if j >= 8 else lane >= 64), 0.0, new)

    sweep(rr2, lr2, ring, band, *EAST, functools.partial(emit, EAST[0]), outside)
    sweep(rr, lr, ring, band, *OUTER, functools.partial(emit, OUTER[0]))
    shipped.wait()
    pltpu.make_async_copy(ob, ob, sem.at[1]).wait()


def spread(tmp, pieces, store):
    size = pieces[0].shape[0]
    for t, piece in enumerate(pieces):
        tmp[pl.ds((size + 1) * t, size), :] = piece
    for u in range(len(pieces) // 8):
        for r in range(size):
            store(r, 8 * u, tmp[pl.ds((size + 1) * 8 * u + r, 8, stride=size + 1), :])


def edge_kernel(x1, x2, partial, late, alias, out, rr, lr, ring, ob, tmp, sem):
    del alias
    shipped = ship(late, out, SECOND, sem.at[0])
    row = lax.axis_index("row")
    odd = (row % 2) == 1
    last = lax.axis_index("col") == lax.axis_size("col") - 1
    north = jnp.where(odd, x1[...], x2[...])
    south = jnp.where(odd, x2[...], x1[...])
    north = jnp.where(row == 0, 0.0, north)
    south = jnp.where(row == lax.axis_size("row") - 1, 0.0, south)
    both = jnp.where(iota((8, 896), 0) >= 4, north, south)
    parts = [both[:, 128 * t : 128 * t + 128] for t in range(7)]
    right = [parts[0], parts[1], parts[2], parts[3], parts[0]]
    left = [parts[4], parts[5], parts[6], parts[4]]
    bases = [16 * t for t in range(16)]
    lay_out(right, left, bases, 16, rr, lr)
    a, b = iota((128, 128), 0), iota((128, 128), 1)
    e, r = a % 8, b % 8
    near = ((e < 4) & (r >= e + 4)) | ((e >= 4) & (r <= e - 4))
    band = one_hot(((a // 8) == (b // 8)) & near)
    band = jnp.concatenate([band, band], axis=1)
    lane = iota((1, 128), 1)
    pieces = []

    def outside(j, new):
        return jnp.where((lane >= 120) & last, 0.0, new) if j >= 20 else new

    def copies(half):
        cols = pl.ds(8 * half, 8)
        source, target = ob.reshape(8, 16, 16, ND), out.reshape(ROWS, 16, 16, ND)
        return [
            pltpu.make_async_copy(source.at[pl.ds(0, 4), :, cols], target.at[pl.ds(0, 4), :, cols], sem.at[1 + half]),
            pltpu.make_async_copy(source.at[pl.ds(4, 4), :, cols], target.at[pl.ds(ROWS - 4, 4), :, cols], sem.at[3 + half]),
        ]

    def emit(k, done):
        pieces.append(done + jnp.concatenate([partial[b + k] for b in bases], axis=0))
        if k % 8 < 7:
            return

        def store(r, u, value):
            ob[r % 8, pl.ds(16 * (r // 8) + k - 7, 8), :] = value

        spread(tmp.at[k // 8], pieces, store)
        pieces.clear()
        for copy in copies(k // 8):
            copy.start()

    sweep(rr, lr, ring, band, bases, 16, emit, outside)
    for copy in [shipped, *copies(0), *copies(1)]:
        copy.wait()


def params(mib):
    return pltpu.CompilerParams(vmem_limit_bytes=mib << 20)


def exchange(x, to):
    rows, cols = lax.axis_size("row"), lax.axis_size("col")
    pairs = []
    for r in range(rows):
        for c in range(cols):
            s, d = to(r, c, rows, cols)
            pairs.append((r * cols + c, s * cols + d))
    return lax.ppermute(x, ("row", "col"), pairs)


def across(r, c, rows, cols):
    d = c + 1 if c % 2 else c - 1
    return (r, d) if 0 <= d < cols else (r ^ 1, c)


def within(r, c, rows, cols):
    return r, c ^ 1


def rows_even(r, c, rows, cols):
    return r ^ 1, c


def rows_odd(r, c, rows, cols):
    s = r + 1 if r % 2 else r - 1
    return (s, c) if 0 <= s < rows else (r, c ^ 1)


def per_device(left, right):
    shape = jax.ShapeDtypeStruct
    packed, images = pl.pallas_call(
        pack_kernel,
        in_specs=[VMEM],
        out_specs=[VMEM] * 2,
        out_shape=[shape((ROWS + 8, 128), F32), shape((ROWS, 2 * COLS), F32)],
        compiler_params=params(1),
        name="pack",
    )(jnp.concatenate([left, right], axis=1))
    cross = exchange(packed, across)
    intra = exchange(pl.pallas_call(copy_kernel, in_specs=[VMEM], out_specs=VMEM, out_shape=shape((ROWS + 8, 128), F32), compiler_params=params(1), name="again")(packed), within)
    volume = shape((ROWS, COLS, ND), F32)
    sides = shape((COLS, 8, ND), F32)

    def blocks(cols):
        return shape((len(cols), ROWS - 8, ND), F32)

    def scratch(*counts):
        sizes = [size for n in counts for size in (n + 135, n + 8)]
        return [pltpu.VMEM((-(-size // 8) * 8, 128), F32) for size in sizes] + [pltpu.VMEM((16, 128, 128), F32)]

    def cost(cols):
        return pl.CostEstimate(
            flops=2 * 128 * 128 * 128 * len(cols), bytes_accessed=len(cols) << 15, transcendentals=0
        )

    ready, edges = pl.pallas_call(
        inner_kernel,
        in_specs=[VMEM],
        out_specs=[VMEM] * 2,
        out_shape=[blocks(BEFORE), sides],
        scratch_shapes=scratch(INNER[1]),
        compiler_params=params(4),
        cost_estimate=cost(BEFORE),
        name="inner",
    )(images)
    send1, send2 = pl.pallas_call(
        rows_kernel,
        in_specs=[VMEM] * 3,
        out_specs=[VMEM] * 2,
        out_shape=[shape((8, 896), F32)] * 2,
        compiler_params=params(1),
        name="pack_rows",
    )(images, cross, intra)
    got1 = exchange(send1, rows_even)
    got2 = exchange(send2, rows_odd)
    out, late, edges = pl.pallas_call(
        outer_kernel,
        in_specs=[VMEM] * 5,
        out_specs=[HBM, VMEM, VMEM],
        out_shape=[volume, blocks(SECOND), sides],
        scratch_shapes=scratch(OUTER[1], EAST[1])
        + [pltpu.VMEM(blocks(FIRST).shape, F32), pltpu.SemaphoreType.DMA((2,))],
        input_output_aliases={4: 2},
        compiler_params=params(8),
        cost_estimate=cost(FIRST + SECOND),
        name="outer",
    )(images, cross, intra, ready, edges)
    return pl.pallas_call(
        edge_kernel,
        in_specs=[VMEM, VMEM, VMEM, VMEM, HBM],
        out_specs=HBM,
        out_shape=volume,
        scratch_shapes=scratch(16)
        + [
            pltpu.VMEM((8, COLS, ND), F32),
            pltpu.VMEM((2, 8 * 129, 128), F32),
            pltpu.SemaphoreType.DMA((5,)),
        ],
        input_output_aliases={4: 0},
        compiler_params=params(6),
        name="edge",
    )(got1, got2, edges, late, out)


def solution(mesh):
    specs = (P("row", "col"), P("row", "col"))
    return jax.shard_map(
        per_device, mesh=mesh, in_specs=specs, out_specs=P("row", "col", None), check_vma=False
    )
```

```python
import functools

import jax
import jax.numpy as jnp
from jax import lax
from jax.experimental import pallas as pl
from jax.experimental.pallas import tpu as pltpu
from jax.sharding import PartitionSpec as P

ND = 128
ROWS = 64
COLS = 256
F32 = jnp.float32
BF16 = jnp.bfloat16
NT = (((1,), (1,)), ((), ()))
SCALE = 1.0 / 81.0
LATE = 40
VMEM = pl.BlockSpec(memory_space=pltpu.VMEM)
HBM = pl.BlockSpec(memory_space=pl.ANY)


def iota(shape, dim):
    return lax.broadcasted_iota(jnp.int32, shape, dim)


def tile(ref, t):
    return ref[:, 128 * t : 128 * t + 128]


def one_hot(mask):
    return jnp.where(mask, 1.0, 0.0).astype(BF16)


def halves(x):
    high = x.astype(BF16)
    low = (x - high.astype(F32)).astype(BF16)
    return jnp.concatenate([high, low], axis=1)


def pick_transposed(chosen, x):
    a = x.astype(BF16)
    rest = x - a.astype(F32)
    b = rest.astype(BF16)
    c = (rest - b.astype(F32)).astype(BF16)
    dot = functools.partial(lax.dot_general, dimension_numbers=NT, preferred_element_type=F32)
    return (dot(chosen, c) + dot(chosen, b)) + dot(chosen, a)


def neighbours(cross, intra):
    c = lax.axis_index("col")
    odd = (c % 2) == 1
    west = jnp.where(odd, intra, cross)
    east = jnp.where(odd, cross, intra)
    west = jnp.where(c == 0, 0.0, west)
    east = jnp.where(c == lax.axis_size("col") - 1, 0.0, east)
    return west, east


def turn(x, left):
    left %= 128
    return pltpu.roll(x, 128 - left, 1) if left else x


def side_tiles(west, east, groups):
    far = jnp.concatenate([west[8 * g : 8 * g + 8] for g in groups], axis=0)
    west, east = west[ROWS:], east[ROWS:]
    lane = iota((8, 128), 1)
    both = jnp.where(lane % 16 >= 8, east, west)
    right = [jnp.where(lane < 4, turn(east, 16 * g), turn(west, 16 * g + 16)) for g in groups]
    left = [turn(both, 16 * g + 8) for g in groups]
    return far, jnp.concatenate(right, axis=0), jnp.concatenate(left, axis=0)


def pack_kernel(both, out, images, ready, edges, rr, lr, ring):
    images[...] = both[...]
    lane = iota((8, 128), 1)
    sides = jnp.zeros((8, 128), F32)
    for g in range(ROWS // 8):
        l0, l1, r0, r1 = [both[8 * g : 8 * g + 8, 128 * t : 128 * t + 128] for t in range(4)]
        out[8 * g : 8 * g + 8, :] = r1
        left = turn(jnp.where(lane >= 124, l1, l0), -8)
        some = jnp.where(lane < 4, r0, jnp.where(lane < 12, left, turn(r0, -16)))
        sides = jnp.where(lane // 16 == g, turn(some, -16 * g), sides)
    out[ROWS:, :] = sides

    @pl.when(waits_long())
    def _():
        inner(both, ready, edges, rr, lr, ring)


def copy_kernel(x, out):
    out[...] = x[...]


def rows_kernel(images, cross, intra, *sends):
    row = lax.axis_index("row")
    west, east = neighbours(cross[...], intra[...])
    low = iota((8, 128), 0) < 4

    def strip(g, mine):
        far, right_edge, left_edge = side_tiles(west, east, [g])
        l0, l1, r0, r1 = [images[8 * g : 8 * g + 8, 128 * t : 128 * t + 128] for t in range(4)]
        pairs = [(right_edge, left_edge), (far, l0), (r0, l1), (r1, l1)]
        return jnp.concatenate([jnp.where(mine, r, pltpu.roll(l, 4, 0)) for r, l in pairs], axis=1)

    top, bottom = strip(0, low), strip(ROWS // 8 - 1, ~low)
    for boundary, send in enumerate(sends):
        send[...] = jnp.where(row == boundary, bottom, top)


def window(tiles, start):
    v, o = divmod(start, 128)
    if o == 0:
        return tiles[v]
    lane = iota(tiles[v].shape, 1)
    return pltpu.roll(jnp.where(lane >= o, tiles[v], tiles[v + 1]), 128 - o, 1)


def lay_out(right, left, bases, n, rr, lr):
    x = [jnp.concatenate([window(right, b + 120), window(right, b + 248)], axis=1) for b in bases]
    size = -(-(n + 135) // 8) * 8
    q, p = iota((size, 256), 0), iota((size, 256), 1)
    rr[pl.ds(0, size), :] = pick_transposed(one_hot(p == n + 139 - q), jnp.concatenate(x, axis=0))
    x = [window(left, b + 124) for b in bases]
    size = -(-(n + 8) // 8) * 8
    q, p = iota((size, 128), 0), iota((size, 128), 1)
    lr[pl.ds(0, size), :] = pick_transposed(one_hot(p == q), jnp.concatenate(x, axis=0))


def own_band():
    a, b = iota((128, 128), 0), iota((128, 128), 1)
    e = a % 64
    i = jnp.where(e < 4, e, jnp.where(e < 8, e + 56, e - 4))
    band = one_hot(((a // 64) == (b // 64)) & (jnp.abs(i - b % 64) <= 4))
    return jnp.concatenate([band, band], axis=1)


def sweep(rr, lr, ring, band, bases, n, emit, outside=None):
    def cost(j):
        new = jnp.abs(lr[j : j + 1, :] - rr[n + 7 - j : n + 135 - j, :])
        if outside is not None:
            new = outside(j, new)
        if j < n - 1:
            ring[j % 16] = new
        return new

    total = cost(0)
    for j in range(1, 8):
        total = total + cost(j)
    for k in range(n):
        total = total + cost(k + 8)
        emit(k, lax.dot_general(band, halves(total), NT, preferred_element_type=F32) * SCALE)
        if k < n - 1:
            total = total - ring[k % 16]


def columns(segments):
    return [b + k for bases, n, ks in segments for k in ks for b in bases]


INNER = ((132, 192), 60)
OUTER = ((0, 66), 66)
EAST = ((252, 254), 2)
FIRST = [*columns([(*EAST, range(2)), (*OUTER, range(OUTER[1] - LATE))])]
SECOND = columns([(*OUTER, range(OUTER[1] - LATE, OUTER[1]))])
BEFORE = columns([(*INNER, range(INNER[1]))])


def ship(blocks, out, cols, sem):
    for o, c in enumerate(cols):
        pltpu.make_async_copy(blocks.at[o], out.at[pl.ds(4, ROWS - 8), c, :], sem).start()
    return pltpu.make_async_copy(blocks, blocks, sem)


def inner(images, ready, edges, rr, lr, ring):
    l0, l1, r0, r1 = [tile(images, t) for t in range(4)]
    bases, n = INNER
    lay_out([r0, r0, r0, r1, r1], [l0, l0, l1, l1], bases, n, rr, lr)

    def emit(k, done):
        for h in range(2):
            edges[bases[h] + k] = done[64 * h : 64 * h + 8]
            ready[2 * k + h] = done[64 * h + 8 : 64 * h + 64]

    sweep(rr, lr, ring, own_band(), bases, n, emit)


def waits_long():
    c = lax.axis_index("col")
    return (c % 16 == 1) & (c > 1)


def inner_kernel(images, begun, part, ready, edges, rr, lr, ring):
    del begun, part

    @pl.when(~waits_long())
    def _():
        inner(images, ready, edges, rr, lr, ring)


def outer_kernel(images, cross, intra, ready, part, out, late, edges, rr, lr, rr2, lr2, ring, ob, sem):
    del part
    shipped = ship(ready, out, BEFORE, sem.at[0])
    last = lax.axis_index("col") == lax.axis_size("col") - 1
    far, right_edge, left_edge = side_tiles(*neighbours(cross[...], intra[...]), range(ROWS // 8))
    l0, l1, r0, r1 = [tile(images, t) for t in range(4)]
    rights = [right_edge, far, r0, r1, right_edge]
    lefts = [left_edge, l0, l1, left_edge]
    band = own_band()
    lay_out(rights, lefts, *OUTER, rr, lr)
    lay_out(rights, lefts, *EAST, rr2, lr2)
    lane = iota((1, 128), 1)

    def emit(bases, k, done):
        for h in range(2):
            c = bases[h] + k
            edges[c] = done[64 * h : 64 * h + 8]
            block = done[64 * h + 8 : 64 * h + 64]
            if c in SECOND:
                late[SECOND.index(c)] = block
            else:
                o = FIRST.index(c)
                ob[o] = block
                pltpu.make_async_copy(ob.at[o], out.at[pl.ds(4, ROWS - 8), c, :], sem.at[1]).start()

    def outside(j, new):
        if j < 6:
            return new
        return jnp.where(last & (lane >= 0 if j >= 8 else lane >= 64), 0.0, new)

    sweep(rr2, lr2, ring, band, *EAST, functools.partial(emit, EAST[0]), outside)
    sweep(rr, lr, ring, band, *OUTER, functools.partial(emit, OUTER[0]))
    shipped.wait()
    pltpu.make_async_copy(ob, ob, sem.at[1]).wait()


def spread(tmp, pieces, store):
    size = pieces[0].shape[0]
    for t, piece in enumerate(pieces):
        tmp[pl.ds((size + 1) * t, size), :] = piece
    for u in range(len(pieces) // 8):
        for r in range(size):
            store(r, 8 * u, tmp[pl.ds((size + 1) * 8 * u + r, 8, stride=size + 1), :])


def edge_kernel(x1, x2, x3, partial, late, alias, out, rr, lr, ring, ob, tmp, sem):
    del alias
    shipped = ship(late, out, SECOND, sem.at[0])
    row = lax.axis_index("row")
    last = lax.axis_index("col") == lax.axis_size("col") - 1
    north = jnp.where(row == 1, x1[...], jnp.where(row == 2, x2[...], jnp.where(row == 3, x3[...], 0.0)))
    south = jnp.where(row == 0, x1[...], jnp.where(row == 1, x2[...], jnp.where(row == 2, x3[...], 0.0)))
    low = iota((8, 512), 0) < 4
    right = jnp.where(low, south, north)
    left = pltpu.roll(jnp.where(low, north, south), 4, 0)
    right = [right[:, 128 * t : 128 * t + 128] for t in (0, 1, 2, 3, 0)]
    left = [left[:, 128 * t : 128 * t + 128] for t in (0, 1, 2, 0)]
    bases = [16 * t for t in range(16)]
    lay_out(right, left, bases, 16, rr, lr)
    a, b = iota((128, 128), 0), iota((128, 128), 1)
    e, r = a % 8, b % 8
    near = ((e < 4) & (r >= e + 4)) | ((e >= 4) & (r <= e - 4))
    band = one_hot(((a // 8) == (b // 8)) & near)
    band = jnp.concatenate([band, band], axis=1)
    lane = iota((1, 128), 1)
    pieces = []

    def outside(j, new):
        return jnp.where((lane >= 120) & last, 0.0, new) if j >= 20 else new

    def copies(half):
        cols = pl.ds(8 * half, 8)
        source, target = ob.reshape(8, 16, 16, ND), out.reshape(ROWS, 16, 16, ND)
        return [
            pltpu.make_async_copy(source.at[pl.ds(0, 4), :, cols], target.at[pl.ds(0, 4), :, cols], sem.at[1 + half]),
            pltpu.make_async_copy(source.at[pl.ds(4, 4), :, cols], target.at[pl.ds(ROWS - 4, 4), :, cols], sem.at[3 + half]),
        ]

    def emit(k, done):
        pieces.append(done + jnp.concatenate([partial[b + k] for b in bases], axis=0))
        if k % 8 < 7:
            return

        def store(r, u, value):
            ob[r % 8, pl.ds(16 * (r // 8) + k - 7, 8), :] = value

        spread(tmp.at[k // 8], pieces, store)
        pieces.clear()
        for copy in copies(k // 8):
            copy.start()

    sweep(rr, lr, ring, band, bases, 16, emit, outside)
    for copy in [shipped, *copies(0), *copies(1)]:
        copy.wait()


def params(mib):
    return pltpu.CompilerParams(vmem_limit_bytes=mib << 20)


def exchange(x, to):
    rows, cols = lax.axis_size("row"), lax.axis_size("col")
    pairs = []
    for r in range(rows):
        for c in range(cols):
            s, d = to(r, c, rows, cols)
            pairs.append((r * cols + c, s * cols + d))
    return lax.ppermute(x, ("row", "col"), pairs)


def across(r, c, rows, cols):
    d = c + 1 if c % 2 else c - 1
    return (r, d) if 0 <= d < cols else (r ^ 1, c)


def within(r, c, rows, cols):
    return r, c ^ 1


def boundary_pairs(boundary):
    other = {boundary: boundary + 1, boundary + 1: boundary}
    return lambda r, c, rows, cols: (other[r], c) if r in other else (r, c ^ 1)


def per_device(left, right):
    shape = jax.ShapeDtypeStruct
    volume = shape((ROWS, COLS, ND), F32)
    sides = shape((COLS, 8, ND), F32)

    def blocks(cols):
        return shape((len(cols), ROWS - 8, ND), F32)

    def scratch(*counts):
        sizes = [size for n in counts for size in (n + 135, n + 8)]
        return [pltpu.VMEM((-(-size // 8) * 8, 128), F32) for size in sizes] + [pltpu.VMEM((16, 128, 128), F32)]

    def cost(cols):
        return pl.CostEstimate(
            flops=2 * 128 * 128 * 128 * len(cols), bytes_accessed=len(cols) << 15, transcendentals=0
        )

    packed, images, ready, edges = pl.pallas_call(
        pack_kernel,
        in_specs=[VMEM],
        out_specs=[VMEM] * 4,
        out_shape=[shape((ROWS + 8, 128), F32), shape((ROWS, 2 * COLS), F32), blocks(BEFORE), sides],
        scratch_shapes=scratch(INNER[1]),
        compiler_params=params(4),
        name="pack",
    )(jnp.concatenate([left, right], axis=1))
    cross = exchange(packed, across)
    intra = exchange(pl.pallas_call(copy_kernel, in_specs=[VMEM], out_specs=VMEM, out_shape=shape((ROWS + 8, 128), F32), compiler_params=params(1), name="again")(packed), within)
    ready, edges = pl.pallas_call(
        inner_kernel,
        in_specs=[VMEM] * 3,
        out_specs=[VMEM] * 2,
        out_shape=[blocks(BEFORE), sides],
        scratch_shapes=scratch(INNER[1]),
        input_output_aliases={1: 0, 2: 1},
        compiler_params=params(4),
        cost_estimate=cost(BEFORE),
        name="inner",
    )(images, ready, edges)
    strip = shape((8, 512), F32)
    sends = pl.pallas_call(
        rows_kernel,
        in_specs=[VMEM] * 3,
        out_specs=[VMEM] * 3,
        out_shape=[strip] * 3,
        compiler_params=params(1),
        name="pack_rows",
    )(images, cross, intra)
    strips = [exchange(send, boundary_pairs(b)) for b, send in enumerate(sends)]
    out, late, edges = pl.pallas_call(
        outer_kernel,
        in_specs=[VMEM] * 5,
        out_specs=[HBM, VMEM, VMEM],
        out_shape=[volume, blocks(SECOND), sides],
        scratch_shapes=scratch(OUTER[1], EAST[1])
        + [pltpu.VMEM(blocks(FIRST).shape, F32), pltpu.SemaphoreType.DMA((2,))],
        input_output_aliases={4: 2},
        compiler_params=params(8),
        cost_estimate=cost(FIRST + SECOND),
        name="outer",
    )(images, cross, intra, ready, edges)
    return pl.pallas_call(
        edge_kernel,
        in_specs=[VMEM] * 5 + [HBM],
        out_specs=HBM,
        out_shape=volume,
        scratch_shapes=scratch(16)
        + [
            pltpu.VMEM((8, COLS, ND), F32),
            pltpu.VMEM((2, 8 * 129, 128), F32),
            pltpu.SemaphoreType.DMA((5,)),
        ],
        input_output_aliases={5: 0},
        compiler_params=params(6),
        name="edge",
    )(*strips, edges, late, out)


def solution(mesh):
    specs = (P("row", "col"), P("row", "col"))
    return jax.shard_map(
        per_device, mesh=mesh, in_specs=specs, out_specs=P("row", "col", None), check_vma=False
    )
```

```python
import functools

import jax
import jax.numpy as jnp
from jax import lax
from jax.experimental import pallas as pl
from jax.experimental.pallas import tpu as pltpu
from jax.sharding import PartitionSpec as P

ND = 128
ROWS = 64
COLS = 256
F32 = jnp.float32
BF16 = jnp.bfloat16
NT = (((1,), (1,)), ((), ()))
SCALE = 1.0 / 81.0
LATE = 40
VMEM = pl.BlockSpec(memory_space=pltpu.VMEM)
HBM = pl.BlockSpec(memory_space=pl.ANY)


def iota(shape, dim):
    return lax.broadcasted_iota(jnp.int32, shape, dim)


def tile(ref, t):
    return ref[:, 128 * t : 128 * t + 128]


def one_hot(mask):
    return jnp.where(mask, 1.0, 0.0).astype(BF16)


def halves(x):
    high = x.astype(BF16)
    low = (x - high.astype(F32)).astype(BF16)
    return jnp.concatenate([high, low], axis=1)


def pick_transposed(chosen, x):
    a = x.astype(BF16)
    rest = x - a.astype(F32)
    b = rest.astype(BF16)
    c = (rest - b.astype(F32)).astype(BF16)
    dot = functools.partial(lax.dot_general, dimension_numbers=NT, preferred_element_type=F32)
    return (dot(chosen, c) + dot(chosen, b)) + dot(chosen, a)


def neighbours(cross, intra):
    c = lax.axis_index("col")
    odd = (c % 2) == 1
    west = jnp.where(odd, intra, cross)
    east = jnp.where(odd, cross, intra)
    west = jnp.where(c == 0, 0.0, west)
    east = jnp.where(c == lax.axis_size("col") - 1, 0.0, east)
    return west, east


def turn(x, left):
    left %= 128
    return pltpu.roll(x, 128 - left, 1) if left else x


def side_tiles(west, east, groups):
    far = jnp.concatenate([west[8 * g : 8 * g + 8] for g in groups], axis=0)
    west, east = west[ROWS:], east[ROWS:]
    lane = iota((8, 128), 1)
    both = jnp.where(lane % 16 >= 8, east, west)
    right = [jnp.where(lane < 4, turn(east, 16 * g), turn(west, 16 * g + 16)) for g in groups]
    left = [turn(both, 16 * g + 8) for g in groups]
    return far, jnp.concatenate(right, axis=0), jnp.concatenate(left, axis=0)


def pack_kernel(both, out, images, ready, edges, rr, lr, ring):
    images[...] = both[...]
    lane = iota((8, 128), 1)
    sides = jnp.zeros((8, 128), F32)
    for g in range(ROWS // 8):
        l0, l1, r0, r1 = [both[8 * g : 8 * g + 8, 128 * t : 128 * t + 128] for t in range(4)]
        out[8 * g : 8 * g + 8, :] = r1
        left = turn(jnp.where(lane >= 124, l1, l0), -8)
        some = jnp.where(lane < 4, r0, jnp.where(lane < 12, left, turn(r0, -16)))
        sides = jnp.where(lane // 16 == g, turn(some, -16 * g), sides)
    out[ROWS:, :] = sides

    @pl.when(waits_long())
    def _():
        inner(both, ready, edges, rr, lr, ring)


def copy_kernel(x, out):
    out[...] = x[...]


def rows_kernel(images, cross, intra, *sends):
    row = lax.axis_index("row")
    west, east = neighbours(cross[...], intra[...])
    low = iota((8, 128), 0) < 4

    def strip(g, mine):
        far, right_edge, left_edge = side_tiles(west, east, [g])
        l0, l1, r0, r1 = [images[8 * g : 8 * g + 8, 128 * t : 128 * t + 128] for t in range(4)]
        pairs = [(right_edge, left_edge), (far, l0), (r0, l1), (r1, l1)]
        return jnp.concatenate([jnp.where(mine, r, pltpu.roll(l, 4, 0)) for r, l in pairs], axis=1)

    top, bottom = strip(0, low), strip(ROWS // 8 - 1, ~low)
    for boundary, send in enumerate(sends):
        send[...] = jnp.where(row == boundary, bottom, top)


def window(tiles, start):
    v, o = divmod(start, 128)
    if o == 0:
        return tiles[v]
    lane = iota(tiles[v].shape, 1)
    return pltpu.roll(jnp.where(lane >= o, tiles[v], tiles[v + 1]), 128 - o, 1)


def lay_out(right, left, bases, n, rr, lr):
    x = [jnp.concatenate([window(right, b + 120), window(right, b + 248)], axis=1) for b in bases]
    size = -(-(n + 135) // 8) * 8
    q, p = iota((size, 256), 0), iota((size, 256), 1)
    rr[pl.ds(0, size), :] = pick_transposed(one_hot(p == n + 139 - q), jnp.concatenate(x, axis=0))
    x = [window(left, b + 124) for b in bases]
    size = -(-(n + 8) // 8) * 8
    q, p = iota((size, 128), 0), iota((size, 128), 1)
    lr[pl.ds(0, size), :] = pick_transposed(one_hot(p == q), jnp.concatenate(x, axis=0))


def own_band():
    a, b = iota((128, 128), 0), iota((128, 128), 1)
    e = a % 64
    i = jnp.where(e < 4, e, jnp.where(e < 8, e + 56, e - 4))
    band = one_hot(((a // 64) == (b // 64)) & (jnp.abs(i - b % 64) <= 4))
    return jnp.concatenate([band, band], axis=1)


def sweep(rr, lr, ring, band, bases, n, emit, outside=None):
    def cost(j):
        new = jnp.abs(lr[j : j + 1, :] - rr[n + 7 - j : n + 135 - j, :])
        if outside is not None:
            new = outside(j, new)
        if j < n - 1:
            ring[j % 16] = new
        return new

    total = cost(0)
    for j in range(1, 8):
        total = total + cost(j)
    for k in range(n):
        total = total + cost(k + 8)
        emit(k, lax.dot_general(band, halves(total), NT, preferred_element_type=F32) * SCALE)
        if k < n - 1:
            total = total - ring[k % 16]


def columns(segments):
    return [b + k for bases, n, ks in segments for k in ks for b in bases]


INNER = ((132, 192), 60)
OUTER = ((0, 66), 66)
EAST = ((252, 254), 2)
FIRST = [*columns([(*EAST, range(2)), (*OUTER, range(OUTER[1] - LATE))])]
SECOND = columns([(*OUTER, range(OUTER[1] - LATE, OUTER[1]))])
BEFORE = columns([(*INNER, range(INNER[1]))])


def ship(blocks, out, cols, sem):
    for o, c in enumerate(cols):
        pltpu.make_async_copy(blocks.at[o], out.at[pl.ds(4, ROWS - 8), c, :], sem).start()
    return pltpu.make_async_copy(blocks, blocks, sem)


def inner(images, ready, edges, rr, lr, ring):
    l0, l1, r0, r1 = [tile(images, t) for t in range(4)]
    bases, n = INNER
    lay_out([r0, r0, r0, r1, r1], [l0, l0, l1, l1], bases, n, rr, lr)

    def emit(k, done):
        for h in range(2):
            edges[bases[h] + k] = done[64 * h : 64 * h + 8]
            ready[2 * k + h] = done[64 * h + 8 : 64 * h + 64]

    sweep(rr, lr, ring, own_band(), bases, n, emit)


def waits_long():
    c = lax.axis_index("col")
    return (c % 16 == 1) & (c > 1)


def inner_kernel(images, begun, part, ready, edges, rr, lr, ring):
    del begun, part

    @pl.when(~waits_long())
    def _():
        inner(images, ready, edges, rr, lr, ring)


def outer_kernel(images, cross, intra, ready, part, out, late, edges, rr, lr, rr2, lr2, ring, ob, sem):
    del part
    shipped = ship(ready, out, BEFORE, sem.at[0])
    last = lax.axis_index("col") == lax.axis_size("col") - 1
    far, right_edge, left_edge = side_tiles(*neighbours(cross[...], intra[...]), range(ROWS // 8))
    l0, l1, r0, r1 = [tile(images, t) for t in range(4)]
    rights = [right_edge, far, r0, r1, right_edge]
    lefts = [left_edge, l0, l1, left_edge]
    band = own_band()
    lay_out(rights, lefts, *OUTER, rr, lr)
    lay_out(rights, lefts, *EAST, rr2, lr2)
    lane = iota((1, 128), 1)

    def emit(bases, k, done):
        for h in range(2):
            c = bases[h] + k
            edges[c] = done[64 * h : 64 * h + 8]
            block = done[64 * h + 8 : 64 * h + 64]
            if c in SECOND:
                late[SECOND.index(c)] = block
            else:
                o = FIRST.index(c)
                ob[o] = block
                pltpu.make_async_copy(ob.at[o], out.at[pl.ds(4, ROWS - 8), c, :], sem.at[1]).start()

    def outside(j, new):
        if j < 6:
            return new
        return jnp.where(last & (lane >= 0 if j >= 8 else lane >= 64), 0.0, new)

    sweep(rr2, lr2, ring, band, *EAST, functools.partial(emit, EAST[0]), outside)
    sweep(rr, lr, ring, band, *OUTER, functools.partial(emit, OUTER[0]))
    shipped.wait()
    pltpu.make_async_copy(ob, ob, sem.at[1]).wait()


def spread(tmp, pieces, store):
    size = pieces[0].shape[0]
    for t, piece in enumerate(pieces):
        tmp[pl.ds((size + 1) * t, size), :] = piece
    for u in range(len(pieces) // 8):
        for r in range(size):
            store(r, 8 * u, tmp[pl.ds((size + 1) * 8 * u + r, 8, stride=size + 1), :])


def edge_kernel(x1, x2, x3, partial, late, alias, out, rr, lr, ring, ob, tmp, sem):
    del alias
    shipped = ship(late, out, SECOND, sem.at[0])
    row = lax.axis_index("row")
    last = lax.axis_index("col") == lax.axis_size("col") - 1
    north = jnp.where(row == 1, x1[...], jnp.where(row == 2, x2[...], jnp.where(row == 3, x3[...], 0.0)))
    south = jnp.where(row == 0, x1[...], jnp.where(row == 1, x2[...], jnp.where(row == 2, x3[...], 0.0)))
    low = iota((8, 512), 0) < 4
    right = jnp.where(low, south, north)
    left = pltpu.roll(jnp.where(low, north, south), 4, 0)
    right = [right[:, 128 * t : 128 * t + 128] for t in (0, 1, 2, 3, 0)]
    left = [left[:, 128 * t : 128 * t + 128] for t in (0, 1, 2, 0)]
    bases = [16 * t for t in range(16)]
    lay_out(right, left, bases, 16, rr, lr)
    a, b = iota((128, 128), 0), iota((128, 128), 1)
    e, r = a % 8, b % 8
    near = ((e < 4) & (r >= e + 4)) | ((e >= 4) & (r <= e - 4))
    band = one_hot(((a // 8) == (b // 8)) & near)
    band = jnp.concatenate([band, band], axis=1)
    lane = iota((1, 128), 1)
    pieces = []

    def outside(j, new):
        return jnp.where((lane >= 120) & last, 0.0, new) if j >= 20 else new

    def copies(half):
        cols = pl.ds(8 * half, 8)
        source, target = ob.reshape(8, 16, 16, ND), out.reshape(ROWS, 16, 16, ND)
        return [
            pltpu.make_async_copy(source.at[pl.ds(0, 4), :, cols], target.at[pl.ds(0, 4), :, cols], sem.at[1 + half]),
            pltpu.make_async_copy(source.at[pl.ds(4, 4), :, cols], target.at[pl.ds(ROWS - 4, 4), :, cols], sem.at[3 + half]),
        ]

    def emit(k, done):
        pieces.append(done + jnp.concatenate([partial[b + k] for b in bases], axis=0))
        if k % 8 < 7:
            return

        def store(r, u, value):
            ob[r % 8, pl.ds(16 * (r // 8) + k - 7, 8), :] = value

        spread(tmp.at[k // 8], pieces, store)
        pieces.clear()
        for copy in copies(k // 8):
            copy.start()

    sweep(rr, lr, ring, band, bases, 16, emit, outside)
    for copy in [shipped, *copies(0), *copies(1)]:
        copy.wait()


def params(mib):
    return pltpu.CompilerParams(vmem_limit_bytes=mib << 20)


def exchange(x, to):
    rows, cols = lax.axis_size("row"), lax.axis_size("col")
    pairs = []
    for r in range(rows):
        for c in range(cols):
            s, d = to(r, c, rows, cols)
            pairs.append((r * cols + c, s * cols + d))
    return lax.ppermute(x, ("row", "col"), pairs)


def across(r, c, rows, cols):
    d = c + 1 if c % 2 else c - 1
    return (r, d) if 0 <= d < cols else (r ^ 1, c)


def within(r, c, rows, cols):
    return r, c ^ 1


def boundary_pairs(boundary):
    other = {boundary: boundary + 1, boundary + 1: boundary}
    return lambda r, c, rows, cols: (other[r], c) if r in other else (r, c ^ 1)


def per_device(left, right):
    shape = jax.ShapeDtypeStruct
    volume = shape((ROWS, COLS, ND), F32)
    sides = shape((COLS, 8, ND), F32)

    def blocks(cols):
        return shape((len(cols), ROWS - 8, ND), F32)

    def scratch(*counts):
        sizes = [size for n in counts for size in (n + 135, n + 8)]
        return [pltpu.VMEM((-(-size // 8) * 8, 128), F32) for size in sizes] + [pltpu.VMEM((16, 128, 128), F32)]

    def cost(cols):
        return pl.CostEstimate(
            flops=2 * 128 * 128 * 128 * len(cols), bytes_accessed=len(cols) << 15, transcendentals=0
        )

    packed, images, ready, edges = pl.pallas_call(
        pack_kernel,
        in_specs=[VMEM],
        out_specs=[VMEM] * 4,
        out_shape=[shape((ROWS + 8, 128), F32), shape((ROWS, 2 * COLS), F32), blocks(BEFORE), sides],
        scratch_shapes=scratch(INNER[1]),
        compiler_params=params(4),
        name="pack",
    )(jnp.concatenate([left, right], axis=1))
    cross = exchange(packed, across)
    intra = exchange(pl.pallas_call(copy_kernel, in_specs=[VMEM], out_specs=VMEM, out_shape=shape((ROWS + 8, 128), F32), compiler_params=params(1), name="again")(packed), within)
    ready, edges = pl.pallas_call(
        inner_kernel,
        in_specs=[VMEM] * 3,
        out_specs=[VMEM] * 2,
        out_shape=[blocks(BEFORE), sides],
        scratch_shapes=scratch(INNER[1]),
        input_output_aliases={1: 0, 2: 1},
        compiler_params=params(4),
        cost_estimate=cost(BEFORE),
        name="inner",
    )(images, ready, edges)
    strip = shape((8, 512), F32)
    sends = pl.pallas_call(
        rows_kernel,
        in_specs=[VMEM] * 3,
        out_specs=[VMEM] * 3,
        out_shape=[strip] * 3,
        compiler_params=params(1),
        name="pack_rows",
    )(images, cross, intra)
    strips = [exchange(send, boundary_pairs(b)) for b, send in enumerate(sends)]
    out, late, edges = pl.pallas_call(
        outer_kernel,
        in_specs=[VMEM] * 5,
        out_specs=[HBM, VMEM, VMEM],
        out_shape=[volume, blocks(SECOND), sides],
        scratch_shapes=scratch(OUTER[1], EAST[1])
        + [pltpu.VMEM(blocks(FIRST).shape, F32), pltpu.SemaphoreType.DMA((2,))],
        input_output_aliases={4: 2},
        compiler_params=params(8),
        cost_estimate=cost(FIRST + SECOND),
        name="outer",
    )(images, cross, intra, ready, edges)
    return pl.pallas_call(
        edge_kernel,
        in_specs=[VMEM] * 5 + [HBM],
        out_specs=HBM,
        out_shape=volume,
        scratch_shapes=scratch(16)
        + [
            pltpu.VMEM((8, COLS, ND), F32),
            pltpu.VMEM((2, 9 * 129, 128), F32),
            pltpu.SemaphoreType.DMA((5,)),
        ],
        input_output_aliases={5: 0},
        compiler_params=params(6),
        name="edge",
    )(*strips, edges, late, out)


def solution(mesh):
    specs = (P("row", "col"), P("row", "col"))
    return jax.shard_map(
        per_device, mesh=mesh, in_specs=specs, out_specs=P("row", "col", None), check_vma=False
    )
```

```python
import functools

import jax
import jax.numpy as jnp
from jax import lax
from jax.experimental import pallas as pl
from jax.experimental.pallas import tpu as pltpu
from jax.sharding import PartitionSpec as P

ND = 128
ROWS = 64
COLS = 256
F32 = jnp.float32
BF16 = jnp.bfloat16
NT = (((1,), (1,)), ((), ()))
SCALE = 1.0 / 81.0
LATE = 40
VMEM = pl.BlockSpec(memory_space=pltpu.VMEM)
HBM = pl.BlockSpec(memory_space=pl.ANY)


def iota(shape, dim):
    return lax.broadcasted_iota(jnp.int32, shape, dim)


def tile(ref, t):
    return ref[:, 128 * t : 128 * t + 128]


def one_hot(mask):
    return jnp.where(mask, 1.0, 0.0).astype(BF16)


def halves(x):
    high = x.astype(BF16)
    low = (x - high.astype(F32)).astype(BF16)
    return jnp.concatenate([high, low], axis=1)


def pick_transposed(chosen, x):
    a = x.astype(BF16)
    rest = x - a.astype(F32)
    b = rest.astype(BF16)
    c = (rest - b.astype(F32)).astype(BF16)
    parts, picks = jnp.concatenate([c, b, a], axis=1), jnp.concatenate([chosen] * 3, axis=1)
    return lax.dot_general(picks, parts, NT, preferred_element_type=F32)


def neighbours(cross, intra):
    c = lax.axis_index("col")
    odd = (c % 2) == 1
    west = jnp.where(odd, intra, cross)
    east = jnp.where(odd, cross, intra)
    west = jnp.where(c == 0, 0.0, west)
    east = jnp.where(c == lax.axis_size("col") - 1, 0.0, east)
    return west, east


def turn(x, left):
    left %= 128
    return pltpu.roll(x, 128 - left, 1) if left else x


def side_tiles(west, east, groups):
    far = jnp.concatenate([west[8 * g : 8 * g + 8] for g in groups], axis=0)
    west, east = west[ROWS:], east[ROWS:]
    lane = iota((8, 128), 1)
    both = jnp.where(lane % 16 >= 8, east, west)
    right = [jnp.where(lane < 4, turn(east, 16 * g), turn(west, 16 * g + 16)) for g in groups]
    left = [turn(both, 16 * g + 8) for g in groups]
    return far, jnp.concatenate(right, axis=0), jnp.concatenate(left, axis=0)


def pack_kernel(both, out, images, ready, edges, rr, lr, ring):
    images[...] = both[...]
    lane = iota((8, 128), 1)
    sides = jnp.zeros((8, 128), F32)
    for g in range(ROWS // 8):
        l0, l1, r0, r1 = [both[8 * g : 8 * g + 8, 128 * t : 128 * t + 128] for t in range(4)]
        out[8 * g : 8 * g + 8, :] = r1
        left = turn(jnp.where(lane >= 124, l1, l0), -8)
        some = jnp.where(lane < 4, r0, jnp.where(lane < 12, left, turn(r0, -16)))
        sides = jnp.where(lane // 16 == g, turn(some, -16 * g), sides)
    out[ROWS:, :] = sides

    @pl.when(waits_long())
    def _():
        inner(both, ready, edges, rr, lr, ring)


def copy_kernel(x, out):
    out[...] = x[...]


def rows_kernel(images, cross, intra, *sends):
    row = lax.axis_index("row")
    west, east = neighbours(cross[...], intra[...])
    low = iota((8, 128), 0) < 4

    def strip(g, mine):
        far, right_edge, left_edge = side_tiles(west, east, [g])
        l0, l1, r0, r1 = [images[8 * g : 8 * g + 8, 128 * t : 128 * t + 128] for t in range(4)]
        pairs = [(right_edge, left_edge), (far, l0), (r0, l1), (r1, l1)]
        return jnp.concatenate([jnp.where(mine, r, pltpu.roll(l, 4, 0)) for r, l in pairs], axis=1)

    top, bottom = strip(0, low), strip(ROWS // 8 - 1, ~low)
    for boundary, send in enumerate(sends):
        send[...] = jnp.where(row == boundary, bottom, top)


def window(tiles, start):
    v, o = divmod(start, 128)
    if o == 0:
        return tiles[v]
    lane = iota(tiles[v].shape, 1)
    return pltpu.roll(jnp.where(lane >= o, tiles[v], tiles[v + 1]), 128 - o, 1)


def lay_out(right, left, bases, n, rr, lr):
    x = [jnp.concatenate([window(right, b + 120), window(right, b + 248)], axis=1) for b in bases]
    size = -(-(n + 135) // 8) * 8
    q, p = iota((size, 256), 0), iota((size, 256), 1)
    rr[pl.ds(0, size), :] = pick_transposed(one_hot(p == n + 139 - q), jnp.concatenate(x, axis=0))
    x = [window(left, b + 124) for b in bases]
    size = -(-(n + 8) // 8) * 8
    q, p = iota((size, 128), 0), iota((size, 128), 1)
    lr[pl.ds(0, size), :] = pick_transposed(one_hot(p == q), jnp.concatenate(x, axis=0))


def own_band():
    a, b = iota((128, 128), 0), iota((128, 128), 1)
    e = a % 64
    i = jnp.where(e < 4, e, jnp.where(e < 8, e + 56, e - 4))
    band = one_hot(((a // 64) == (b // 64)) & (jnp.abs(i - b % 64) <= 4))
    return jnp.concatenate([band, band], axis=1)


def sweep(rr, lr, ring, band, bases, n, emit, outside=None):
    def cost(j):
        new = jnp.abs(lr[j : j + 1, :] - rr[n + 7 - j : n + 135 - j, :])
        if outside is not None:
            new = outside(j, new)
        if j < n - 1:
            ring[j % 16] = new
        return new

    total = cost(0)
    for j in range(1, 8):
        total = total + cost(j)
    for k in range(n):
        total = total + cost(k + 8)
        emit(k, lax.dot_general(band, halves(total), NT, preferred_element_type=F32) * SCALE)
        if k < n - 1:
            total = total - ring[k % 16]


def columns(segments):
    return [b + k for bases, n, ks in segments for k in ks for b in bases]


INNER = ((132, 192), 60)
OUTER = ((0, 66), 66)
EAST = ((252, 254), 2)
FIRST = [*columns([(*EAST, range(2)), (*OUTER, range(OUTER[1] - LATE))])]
SECOND = columns([(*OUTER, range(OUTER[1] - LATE, OUTER[1]))])
BEFORE = columns([(*INNER, range(INNER[1]))])


def ship(blocks, out, cols, sem):
    for o, c in enumerate(cols):
        pltpu.make_async_copy(blocks.at[o], out.at[pl.ds(4, ROWS - 8), c, :], sem).start()
    return pltpu.make_async_copy(blocks, blocks, sem)


def inner(images, ready, edges, rr, lr, ring):
    l0, l1, r0, r1 = [tile(images, t) for t in range(4)]
    bases, n = INNER
    lay_out([r0, r0, r0, r1, r1], [l0, l0, l1, l1], bases, n, rr, lr)

    def emit(k, done):
        for h in range(2):
            edges[bases[h] + k] = done[64 * h : 64 * h + 8]
            ready[2 * k + h] = done[64 * h + 8 : 64 * h + 64]

    sweep(rr, lr, ring, own_band(), bases, n, emit)


def waits_long():
    c = lax.axis_index("col")
    return (c % 16 == 1) & (c > 1)


def inner_kernel(images, begun, part, ready, edges, rr, lr, ring):
    del begun, part

    @pl.when(~waits_long())
    def _():
        inner(images, ready, edges, rr, lr, ring)


def outer_kernel(images, cross, intra, ready, part, out, late, edges, rr, lr, rr2, lr2, ring, ob, sem):
    del part
    shipped = ship(ready, out, BEFORE, sem.at[0])
    last = lax.axis_index("col") == lax.axis_size("col") - 1
    far, right_edge, left_edge = side_tiles(*neighbours(cross[...], intra[...]), range(ROWS // 8))
    l0, l1, r0, r1 = [tile(images, t) for t in range(4)]
    rights = [right_edge, far, r0, r1, right_edge]
    lefts = [left_edge, l0, l1, left_edge]
    band = own_band()
    lay_out(rights, lefts, *OUTER, rr, lr)
    lay_out(rights, lefts, *EAST, rr2, lr2)
    lane = iota((1, 128), 1)

    def emit(bases, k, done):
        for h in range(2):
            c = bases[h] + k
            edges[c] = done[64 * h : 64 * h + 8]
            block = done[64 * h + 8 : 64 * h + 64]
            if c in SECOND:
                late[SECOND.index(c)] = block
            else:
                o = FIRST.index(c)
                ob[o] = block
                pltpu.make_async_copy(ob.at[o], out.at[pl.ds(4, ROWS - 8), c, :], sem.at[1]).start()

    def outside(j, new):
        if j < 6:
            return new
        return jnp.where(last & (lane >= 0 if j >= 8 else lane >= 64), 0.0, new)

    sweep(rr2, lr2, ring, band, *EAST, functools.partial(emit, EAST[0]), outside)
    sweep(rr, lr, ring, band, *OUTER, functools.partial(emit, OUTER[0]))
    shipped.wait()
    pltpu.make_async_copy(ob, ob, sem.at[1]).wait()


def spread(tmp, pieces, store):
    size = pieces[0].shape[0]
    for t, piece in enumerate(pieces):
        tmp[pl.ds((size + 1) * t, size), :] = piece
    for u in range(len(pieces) // 8):
        for r in range(size):
            store(r, 8 * u, tmp[pl.ds((size + 1) * 8 * u + r, 8, stride=size + 1), :])


def edge_kernel(x1, x2, x3, partial, late, alias, out, rr, lr, ring, ob, tmp, sem):
    del alias
    shipped = ship(late, out, SECOND, sem.at[0])
    row = lax.axis_index("row")
    last = lax.axis_index("col") == lax.axis_size("col") - 1
    north = jnp.where(row == 1, x1[...], jnp.where(row == 2, x2[...], jnp.where(row == 3, x3[...], 0.0)))
    south = jnp.where(row == 0, x1[...], jnp.where(row == 1, x2[...], jnp.where(row == 2, x3[...], 0.0)))
    low = iota((8, 512), 0) < 4
    right = jnp.where(low, south, north)
    left = pltpu.roll(jnp.where(low, north, south), 4, 0)
    right = [right[:, 128 * t : 128 * t + 128] for t in (0, 1, 2, 3, 0)]
    left = [left[:, 128 * t : 128 * t + 128] for t in (0, 1, 2, 0)]
    bases = [16 * t for t in range(16)]
    lay_out(right, left, bases, 16, rr, lr)
    a, b = iota((128, 128), 0), iota((128, 128), 1)
    e, r = a % 8, b % 8
    near = ((e < 4) & (r >= e + 4)) | ((e >= 4) & (r <= e - 4))
    band = one_hot(((a // 8) == (b // 8)) & near)
    band = jnp.concatenate([band, band], axis=1)
    lane = iota((1, 128), 1)
    pieces = []

    def outside(j, new):
        return jnp.where((lane >= 120) & last, 0.0, new) if j >= 20 else new

    def copies(half):
        cols = pl.ds(8 * half, 8)
        source, target = ob.reshape(8, 16, 16, ND), out.reshape(ROWS, 16, 16, ND)
        return [
            pltpu.make_async_copy(source.at[pl.ds(0, 4), :, cols], target.at[pl.ds(0, 4), :, cols], sem.at[1 + half]),
            pltpu.make_async_copy(source.at[pl.ds(4, 4), :, cols], target.at[pl.ds(ROWS - 4, 4), :, cols], sem.at[3 + half]),
        ]

    def emit(k, done):
        pieces.append(done + jnp.concatenate([partial[b + k] for b in bases], axis=0))
        if k % 8 < 7:
            return

        def store(r, u, value):
            ob[r % 8, pl.ds(16 * (r // 8) + k - 7, 8), :] = value

        spread(tmp.at[k // 8], pieces, store)
        pieces.clear()
        for copy in copies(k // 8):
            copy.start()

    sweep(rr, lr, ring, band, bases, 16, emit, outside)
    for copy in [shipped, *copies(0), *copies(1)]:
        copy.wait()


def params(mib):
    return pltpu.CompilerParams(vmem_limit_bytes=mib << 20)


def exchange(x, to):
    rows, cols = lax.axis_size("row"), lax.axis_size("col")
    pairs = []
    for r in range(rows):
        for c in range(cols):
            s, d = to(r, c, rows, cols)
            pairs.append((r * cols + c, s * cols + d))
    return lax.ppermute(x, ("row", "col"), pairs)


def across(r, c, rows, cols):
    d = c + 1 if c % 2 else c - 1
    return (r, d) if 0 <= d < cols else (r ^ 1, c)


def within(r, c, rows, cols):
    return r, c ^ 1


def boundary_pairs(boundary):
    other = {boundary: boundary + 1, boundary + 1: boundary}
    return lambda r, c, rows, cols: (other[r], c) if r in other else (r, c ^ 1)


def per_device(left, right):
    shape = jax.ShapeDtypeStruct
    volume = shape((ROWS, COLS, ND), F32)
    sides = shape((COLS, 8, ND), F32)

    def blocks(cols):
        return shape((len(cols), ROWS - 8, ND), F32)

    def scratch(*counts):
        sizes = [size for n in counts for size in (n + 135, n + 8)]
        return [pltpu.VMEM((-(-size // 8) * 8, 128), F32) for size in sizes] + [pltpu.VMEM((16, 128, 128), F32)]

    def cost(cols):
        return pl.CostEstimate(
            flops=2 * 128 * 128 * 128 * len(cols), bytes_accessed=len(cols) << 15, transcendentals=0
        )

    packed, images, ready, edges = pl.pallas_call(
        pack_kernel,
        in_specs=[VMEM],
        out_specs=[VMEM] * 4,
        out_shape=[shape((ROWS + 8, 128), F32), shape((ROWS, 2 * COLS), F32), blocks(BEFORE), sides],
        scratch_shapes=scratch(INNER[1]),
        compiler_params=params(4),
        name="pack",
    )(jnp.concatenate([left, right], axis=1))
    cross = exchange(packed, across)
    intra = exchange(pl.pallas_call(copy_kernel, in_specs=[VMEM], out_specs=VMEM, out_shape=shape((ROWS + 8, 128), F32), compiler_params=params(1), name="again")(packed), within)
    ready, edges = pl.pallas_call(
        inner_kernel,
        in_specs=[VMEM] * 3,
        out_specs=[VMEM] * 2,
        out_shape=[blocks(BEFORE), sides],
        scratch_shapes=scratch(INNER[1]),
        input_output_aliases={1: 0, 2: 1},
        compiler_params=params(4),
        cost_estimate=cost(BEFORE),
        name="inner",
    )(images, ready, edges)
    strip = shape((8, 512), F32)
    sends = pl.pallas_call(
        rows_kernel,
        in_specs=[VMEM] * 3,
        out_specs=[VMEM] * 3,
        out_shape=[strip] * 3,
        compiler_params=params(1),
        name="pack_rows",
    )(images, cross, intra)
    strips = [exchange(send, boundary_pairs(b)) for b, send in enumerate(sends)]
    out, late, edges = pl.pallas_call(
        outer_kernel,
        in_specs=[VMEM] * 5,
        out_specs=[HBM, VMEM, VMEM],
        out_shape=[volume, blocks(SECOND), sides],
        scratch_shapes=scratch(OUTER[1], EAST[1])
        + [pltpu.VMEM(blocks(FIRST).shape, F32), pltpu.SemaphoreType.DMA((2,))],
        input_output_aliases={4: 2},
        compiler_params=params(8),
        cost_estimate=cost(FIRST + SECOND),
        name="outer",
    )(images, cross, intra, ready, edges)
    return pl.pallas_call(
        edge_kernel,
        in_specs=[VMEM] * 5 + [HBM],
        out_specs=HBM,
        out_shape=volume,
        scratch_shapes=scratch(16)
        + [
            pltpu.VMEM((8, COLS, ND), F32),
            pltpu.VMEM((2, 9 * 129, 128), F32),
            pltpu.SemaphoreType.DMA((5,)),
        ],
        input_output_aliases={5: 0},
        compiler_params=params(6),
        name="edge",
    )(*strips, edges, late, out)


def solution(mesh):
    specs = (P("row", "col"), P("row", "col"))
    return jax.shard_map(
        per_device, mesh=mesh, in_specs=specs, out_specs=P("row", "col", None), check_vma=False
    )
```
